256 devices in a mesh: seg: 16 (over x_lo, y, core), grp: 16 (over x_hi, z).
Axes of the slice: x: 4 (x_hi: 2, x_lo: 2; x = x_hi * 2 + x_lo), y: 4, z: 8, core: 2. Of those that a mesh axis runs over, the one named last changes fastest.
Arguments:
- strain: bfloat16 [32768, 1792], P(('seg', 'grp')), may hold values from -40 to 40
- counts: int32 [32768], P(('seg', 'grp')), may hold values from 448 to 1792, as said below
- working: int32 [32768], P(('seg', 'grp')), may hold values 0 or 1
- mixing: bfloat16 [2048, 2048], P('grp'), may hold values from -0.125 to 0.125
- owners: int32 [2], replicated, may hold values from 0 to 255
- offsets: int32 [2], replicated, may hold values from 0 to 64
Outputs:
- correlations: bfloat16 [2, 201, 64, 32768], P(None, None, None, ('seg', 'grp'))
The draws below stay inside these ranges and needn't reach their ends.
Inputs may be any that keep to these rules, and one draw needn't show every extreme that they name: `counts`: some channel has 1792 valid samples in every draw.
All inputs are finite; a program needn't handle non-finite values. No bound on the sum of `working` on one device may be relied on, other than what follows from the above.
Results may differ from the reference program's by a relative error of at most 0.0058.
Values may be sent and summed in bfloat16 or wider, within the bound.
No kernel may reach another device: no remote copies, remote signals or barrier semaphores. Data moves between devices by JAX's collectives and lax.ppermute only.
A program may use at most 64 MiB of HBM per device.

```python
import math
import jax
import jax.numpy as jnp
from jax import lax

CH_DEV = 128
NS = 1792
SRC = 64
LAG = 100
ROUNDS = 2
LAGS = 201
SEG_CH = 2048
CHANNELS = 32768


def draw_strain(key, part):
    key = jax.random.fold_in(key, 7)
    base_key, channel_key, time_key = jax.random.split(key, 3)
    base = jnp.clip(jax.random.normal(base_key, (CHANNELS, NS), jnp.float32), -4.0, 4.0)
    top = 10.0
    channel_scale = 0.3 * jnp.exp(jax.random.uniform(channel_key, (CHANNELS, 1), jnp.float32, 0.0, math.log(10.0)))
    width = max(NS // 64, 1)
    pieces = NS // width
    time_scale = 0.3 * jnp.exp(jax.random.uniform(time_key, (1, pieces), jnp.float32, 0.0, math.log(top)))
    time_scale = jnp.repeat(time_scale, width, axis=1)
    return (base * channel_scale * time_scale).astype(jnp.bfloat16)


def draw_counts(key, part):
    key = jax.random.fold_in(key, 11)
    device_key, extra_key, full_key = jax.random.split(key, 3)
    devices = CHANNELS // CH_DEV
    device_weight = jax.random.randint(device_key, (devices,), 1, 5)
    extra = jax.random.randint(extra_key, (CHANNELS,), 0, NS - NS // 4 + 1)
    counts = NS // 4 + extra * jnp.repeat(device_weight, CH_DEV) // 4
    full_index = jax.random.randint(full_key, (), 0, CHANNELS)
    counts = counts.at[full_index].set(NS)
    return counts.astype(jnp.int32)


def with_ends(array, key, least, top_value):
    longest = array.shape.index(max(array.shape))
    spots = []
    for shift in (0, 1):
        where = [jax.random.randint(jax.random.fold_in(key, axis), (), 0, length) for axis, length in enumerate(array.shape)]
        where[longest] = (where[longest] + shift) % array.shape[longest]
        spots.append(tuple(where))
    return array.at[spots[0]].set(least).at[spots[1]].set(top_value)


def shard_levels(rng, extent, cuts, least, top_value):
    gain = 1.0
    for position, blocks in cuts:
        draws = jax.random.uniform(jax.random.fold_in(jax.random.fold_in(rng, 6), position), (blocks,), jnp.float32, least / len(cuts), top_value / len(cuts))
        gain = gain * jnp.repeat(jnp.exp(draws), extent[position] // blocks).reshape((-1,) + (1,) * (len(extent) - 1 - position))
    return gain


def centred(key, dims, scale, most, cuts=(), kind=jnp.bfloat16):
    array = scale * jax.random.normal(key, dims, jnp.float32)
    if cuts:
        array = array * shard_levels(key, dims, cuts, -0.22, 0.18)
    return jnp.clip(array, -most, most).astype(kind)


def setup_inputs(seed: int = 0) -> dict:
    key_list = jax.random.split(jax.random.key(seed), 7)
    strain = draw_strain(jax.random.fold_in(key_list[6], 71), 0)
    counts = draw_counts(jax.random.fold_in(key_list[6], 71), 0)
    working = with_ends((jax.random.randint(key_list[2], (CHANNELS,), 0, 16) < 15).astype(jnp.int32), jax.random.fold_in(key_list[2], 1), 0, 1)
    mixing = centred(key_list[3], (SEG_CH, SEG_CH), SEG_CH ** -0.5, 0.125, ((0, 16),))
    owners = jax.random.randint(key_list[4], (ROUNDS,), 0, CHANNELS // CH_DEV).astype(jnp.int32)
    offsets = jax.random.randint(key_list[5], (ROUNDS,), 0, CH_DEV - SRC + 1).astype(jnp.int32)
    return {"strain": strain, "counts": counts, "working": working, "mixing": mixing, "owners": owners, "offsets": offsets}


epsilon = 1e-05

def reference(strain, counts, working, mixing, owners, offsets):
    groups = CHANNELS // SEG_CH
    positions = jnp.arange(NS, dtype=jnp.int32)
    usable = (positions[None, :] < counts[:, None]) & (working[:, None] > 0)
    masked = jnp.where(usable, strain, jnp.zeros_like(strain))
    blocks = masked.reshape(groups, SEG_CH, NS)

    def couple(group_block):
        return jnp.dot(mixing, group_block, preferred_element_type=jnp.float32)
    coupled = lax.map(couple, blocks).reshape(CHANNELS, NS)
    filtered = jnp.where(usable, masked.astype(jnp.float32) - coupled, jnp.float32(0.0))
    sumsq = lax.optimization_barrier(jnp.sum(filtered * filtered, axis=1))
    spread = jnp.sqrt(sumsq / counts.astype(jnp.float32) + epsilon)
    whitened = (filtered / spread[:, None]).astype(jnp.bfloat16)
    norm_scale = 1.0 / float(NS) ** 0.5
    rounds_out = []
    for round_index in range(ROUNDS):
        start_row = (owners[round_index] * CH_DEV + offsets[round_index]).astype(jnp.int32)
        zero_index = jnp.zeros((), jnp.int32)
        source = lax.dynamic_slice(whitened, (start_row, zero_index), (SRC, NS))
        source_pad = jnp.pad(source, ((0, 0), (LAG, LAG)))

        def one_lag(lag_index):
            shifted = lax.dynamic_slice_in_dim(source_pad, lag_index, NS, 1)
            products = jnp.dot(shifted, whitened.T, preferred_element_type=jnp.float32)
            return (products * norm_scale).astype(jnp.bfloat16)
        rounds_out.append(lax.map(one_lag, jnp.arange(LAGS, dtype=jnp.int32)))
    return jnp.stack(rounds_out)
```

```python
import jax
import jax.numpy as jnp
from jax import lax
from jax.experimental import pallas as pl
from jax.experimental.pallas import tpu as pltpu
from jax.sharding import PartitionSpec as P

SRC = 64
LAG = 100
ROUNDS = 2
LAGS = 201
DEPTH = 8
FINE = 13
COARSE = 8
PAIR = 2

epsilon = 1e-05

ACROSS = [(a * DEPTH + z, (1 - a) * DEPTH + z) for a in range(2) for z in range(DEPTH)]
UP = [(a * DEPTH + z, a * DEPTH + (z + 1) % DEPTH) for a in range(2) for z in range(DEPTH)]
DOWN = [(a * DEPTH + z, a * DEPTH + (z - 1) % DEPTH) for a in range(2) for z in range(DEPTH)]


def correlate_kernel(channel_ref, source_ref, out_ref, turned_ref, left_ref, right_ref):
    step = pl.program_id(0)
    rows, samples = source_ref.shape
    channels = channel_ref.shape[0]
    span = FINE * COARSE
    half_steps = COARSE // PAIR

    @pl.when(step == 0)
    def _():
        turned_ref[...] = jnp.zeros_like(turned_ref)
        turned_ref[span : span + samples, :] = channel_ref[...].astype(jnp.float32).T

    def build(first):
        padded = jnp.concatenate(
            [source_ref[...].astype(jnp.float32), jnp.zeros((rows, 128), jnp.float32)], axis=1
        )
        for fine in range(FINE):
            ahead = first + fine
            moved = pltpu.roll(padded, (-ahead) % (samples + 128), axis=1) if ahead else padded
            left_ref[fine * rows : (fine + 1) * rows, :] = moved[:, :samples].astype(jnp.bfloat16)

    @pl.when(step == 0)
    def _():
        build(1 - FINE)

    @pl.when(step == half_steps)
    def _():
        build(1)

    low = step < half_steps
    part = lax.rem(step, half_steps)
    for half in range(PAIR):
        coarse = FINE * (part * PAIR + half)
        start = jnp.where(low, span + coarse, span - coarse)
        right_ref[:, half * channels : (half + 1) * channels] = turned_ref[
            pl.ds(start, samples), :
        ].astype(jnp.bfloat16)
    products = jnp.dot(left_ref[...], right_ref[...], preferred_element_type=jnp.float32)
    scaled = (products * (1.0 / float(samples) ** 0.5)).astype(jnp.bfloat16)
    for half in range(PAIR):
        coarse = FINE * (part * PAIR + half)
        first = jnp.where(low, LAG + 1 - FINE - coarse, LAG + 1 + coarse)
        for fine in range(FINE):
            lag = first + fine

            @pl.when((lag >= 0) & (lag < LAGS))
            def _():
                for r in range(ROUNDS):
                    top = fine * rows + r * SRC
                    out_ref[r, lag] = scaled[top : top + SRC, half * channels : (half + 1) * channels]


def correlate(whitened, sources):
    channels, samples = whitened.shape
    rows = sources.shape[0]
    span = FINE * COARSE
    return pl.pallas_call(
        correlate_kernel,
        grid=(2 * COARSE // PAIR,),
        out_shape=jax.ShapeDtypeStruct((ROUNDS, LAGS, SRC, channels), jnp.bfloat16),
        in_specs=[
            pl.BlockSpec((channels, samples), lambda i: (0, 0)),
            pl.BlockSpec((rows, samples), lambda i: (0, 0)),
        ],
        out_specs=pl.BlockSpec((ROUNDS, LAGS, SRC, channels), lambda i: (0, 0, 0, 0)),
        scratch_shapes=[
            pltpu.VMEM((samples + 2 * span, channels), jnp.float32),
            pltpu.VMEM((FINE * rows, samples), jnp.bfloat16),
            pltpu.VMEM((samples, PAIR * channels), jnp.bfloat16),
        ],
        compiler_params=pltpu.CompilerParams(vmem_limit_bytes=56 * 2**20),
        cost_estimate=pl.CostEstimate(
            flops=2 * LAGS * rows * channels * samples, bytes_accessed=8 * 2**20, transcendentals=0
        ),
    )(whitened, sources)


def everyone(block, axis):
    copies = lax.axis_size(axis)
    tiled = jnp.broadcast_to(block[None], (copies,) + block.shape)
    return lax.all_to_all(tiled, axis, 0, 0)


def on_device(strain, counts, working, mixing, owners, offsets):
    channels, samples = strain.shape
    part = samples // 2
    seg = lax.axis_index("seg")
    grp = lax.axis_index("grp")
    side, level = grp // DEPTH, grp % DEPTH

    facts = jnp.stack([counts, working])
    facts = jnp.concatenate([facts, lax.ppermute(facts, "grp", ACROSS)], axis=1)
    counts2, working2 = facts[0], facts[1]
    positions = lax.broadcasted_iota(jnp.int32, strain.shape, 1)
    usable = (positions < counts[:, None]) & (working[:, None] > 0)
    masked = jnp.where(usable, strain, jnp.zeros_like(strain))
    first, second = masked[:, :part], masked[:, part:]
    mine = jnp.where(side == 0, first, second)
    theirs = jnp.where(side == 0, second, first)
    block = jnp.concatenate([mine, lax.ppermute(theirs, "grp", ACROSS)])
    mixing2 = jnp.concatenate([mixing, lax.ppermute(mixing, "grp", ACROSS)])

    def weights(away, who):
        at = (jnp.where(who == 0, side, 1 - side) * DEPTH + (level + away) % DEPTH) * channels
        return lax.dynamic_slice_in_dim(mixing2, at, channels, 1)

    def term(away, rows, who=None):
        if who is None:
            left = jnp.concatenate([weights(away, 0), weights(away, 1)], axis=1)
        else:
            left = weights(away, who)
        return jnp.dot(left, rows, preferred_element_type=jnp.float32)

    coupled = term(0, block)
    up, down = block, block
    for hop in range(1, DEPTH // 2):
        up = lax.ppermute(up, "grp", UP)
        down = lax.ppermute(down, "grp", DOWN)
        coupled = coupled + term(-hop, up) + term(hop, down)
    up = lax.ppermute(up[:channels], "grp", UP)
    down = lax.ppermute(down[channels:], "grp", DOWN)
    coupled = coupled + term(DEPTH // 2, up, 0) + term(DEPTH // 2, down, 1)

    places = side * part + lax.broadcasted_iota(jnp.int32, block.shape, 1)
    usable2 = (places < counts2[:, None]) & (working2[:, None] > 0)
    filtered = jnp.where(usable2, block.astype(jnp.float32) - coupled, jnp.float32(0.0))
    sums = jnp.sum(filtered * filtered, axis=1)
    sums = sums + jnp.roll(lax.ppermute(sums, "grp", ACROSS), channels)
    spread = jnp.sqrt(sums / counts2.astype(jnp.float32) + epsilon)
    white = (filtered / spread[:, None]).astype(jnp.bfloat16)

    returned = lax.ppermute(white[channels:], "grp", ACROSS)
    picked = []
    for r in range(ROUNDS):
        owner_seg, owner_grp = owners[r] // 16, owners[r] % 16
        row = jnp.where(owner_grp // DEPTH == side, 0, channels) + offsets[r]
        rows = lax.dynamic_slice_in_dim(white, row, SRC, 0)
        here = (owner_seg == seg) & (owner_grp % DEPTH == level)
        picked.append(jnp.where(here, rows, jnp.zeros_like(rows)))
    segs = lax.axis_size("seg")
    sources = jnp.concatenate(picked).reshape(segs, ROUNDS * SRC // segs, part)
    sources = jnp.sum(lax.all_to_all(sources, "seg", 0, 0), axis=0)
    sources = everyone(sources, "grp").reshape(2, DEPTH, ROUNDS * SRC // segs, part)
    sources = jnp.sum(sources, axis=1)
    sources = jnp.concatenate([sources[0], sources[1]], axis=1)
    sources = everyone(sources, "seg").reshape(ROUNDS * SRC, samples)

    kept = white[:channels]
    whitened = jnp.concatenate(
        [jnp.where(side == 0, kept, returned), jnp.where(side == 0, returned, kept)], axis=1
    )
    return correlate(whitened, sources)


def solution(mesh):
    in_specs = (
        P(("seg", "grp"), None),
        P(("seg", "grp")),
        P(("seg", "grp")),
        P("grp", None),
        P(),
        P(),
    )
    out_specs = P(None, None, None, ("seg", "grp"))
    return jax.shard_map(
        on_device, mesh=mesh, in_specs=in_specs, out_specs=out_specs, check_vma=False
    )
```

```python
import jax
import jax.numpy as jnp
from jax import lax
from jax.experimental import pallas as pl
from jax.experimental.pallas import tpu as pltpu
from jax.sharding import PartitionSpec as P

SRC = 64
LAG = 100
ROUNDS = 2
LAGS = 201
DEPTH = 8
FINE = 13
COARSE = 8
CHUNK = 2
SPAN = FINE * COARSE

epsilon = 1e-05

CORES = [(s, s ^ 1) for s in range(16)]
ACROSS = [(a * DEPTH + z, (1 - a) * DEPTH + z) for a in range(2) for z in range(DEPTH)]
UP = [(a * DEPTH + z, a * DEPTH + (z + 1) % DEPTH) for a in range(2) for z in range(DEPTH)]
DOWN = [(a * DEPTH + z, a * DEPTH + (z - 1) % DEPTH) for a in range(2) for z in range(DEPTH)]


def correlate_kernel(
    channel_ref, source_ref, out_ref, turned_ref, left_ref, right_ref, stage_ref, sems
):
    rows = source_ref.shape[0]
    channels, samples = channel_ref.shape
    scales = source_ref[:, samples:].astype(jnp.float32)
    scale = (scales[:, :1] + scales[:, 127:]) * (1.0 / float(samples) ** 0.5)
    turned_ref[:SPAN, :] = jnp.zeros((SPAN, channels), jnp.float32)
    turned_ref[SPAN + samples :, :] = jnp.zeros((SPAN, channels), jnp.float32)
    turned_ref[SPAN : SPAN + samples, :] = channel_ref[...].astype(jnp.float32).T

    def place_sources(side):
        padded = jnp.concatenate(
            [source_ref[:, :samples].astype(jnp.float32), jnp.zeros((rows, 128), jnp.float32)],
            axis=1,
        )
        for fine in range(FINE):
            ahead = fine + (1 if side else 1 - FINE)
            moved = pltpu.roll(padded, (-ahead) % (samples + 128), axis=1) if ahead else padded
            left_ref[side, fine * rows : (fine + 1) * rows, :] = moved[:, :samples].astype(
                jnp.bfloat16
            )

    def place_channels(side):
        for coarse in range(COARSE):
            start = SPAN + FINE * (-coarse if side else coarse)
            right_ref[side, :, coarse * channels : (coarse + 1) * channels] = turned_ref[
                start : start + samples, :
            ].astype(jnp.bfloat16)

    def copies(side, begin, some):
        made = []
        for coarse in range(COARSE):
            at = (coarse if side else COARSE - 1 - coarse) * FINE + begin
            lag = at + (LAG + 1 if side else LAG + 1 - SPAN)
            skip, end = max(0, -lag), min(some, LAGS - lag)
            for r in range(ROUNDS if end > skip else 0):
                made.append(
                    pltpu.make_async_copy(
                        stage_ref.at[side, r, pl.ds(at + skip, end - skip)],
                        out_ref.at[r, pl.ds(lag + skip, end - skip)],
                        sems.at[side, r],
                    )
                )
        return made

    place_sources(0)
    place_channels(0)
    for side in range(2):
        for begin in range(0, FINE, CHUNK):
            some = min(CHUNK, FINE - begin)
            products = jnp.dot(
                left_ref[side, begin * rows : (begin + some) * rows, :],
                right_ref[side],
                preferred_element_type=jnp.float32,
            )
            scaled = (products * jnp.concatenate([scale] * some)).astype(jnp.bfloat16)
            for coarse in range(COARSE):
                for fine in range(begin, begin + some):
                    at = (coarse if side else COARSE - 1 - coarse) * FINE + fine
                    for r in range(ROUNDS):
                        top = (fine - begin) * rows + r * SRC
                        stage_ref[side, r, at] = scaled[
                            top : top + SRC, coarse * channels : (coarse + 1) * channels
                        ]
            for copy in copies(side, begin, some):
                copy.start()
        if side == 0:
            place_sources(1)
            place_channels(1)
    for side in range(2):
        for begin in range(0, FINE, CHUNK):
            for copy in copies(side, begin, min(CHUNK, FINE - begin)):
                copy.wait()


def correlate(whitened, sources):
    channels, samples = whitened.shape
    rows = sources.shape[0]
    return pl.pallas_call(
        correlate_kernel,
        out_shape=jax.ShapeDtypeStruct((ROUNDS, LAGS, SRC, channels), jnp.bfloat16),
        in_specs=[pl.BlockSpec(memory_space=pltpu.VMEM)] * 2,
        out_specs=pl.BlockSpec(memory_space=pl.ANY),
        scratch_shapes=[
            pltpu.VMEM((samples + 2 * SPAN, channels), jnp.float32),
            pltpu.VMEM((2, FINE * rows, samples), jnp.bfloat16),
            pltpu.VMEM((2, samples, COARSE * channels), jnp.bfloat16),
            pltpu.VMEM((2, ROUNDS, SPAN, SRC, channels), jnp.bfloat16),
            pltpu.SemaphoreType.DMA((2, ROUNDS)),
        ],
        compiler_params=pltpu.CompilerParams(vmem_limit_bytes=56 * 2**20),
        cost_estimate=pl.CostEstimate(
            flops=2 * LAGS * rows * channels * samples, bytes_accessed=8 * 2**20, transcendentals=0
        ),
    )(whitened, sources)


def everyone(block, axis):
    copies = lax.axis_size(axis)
    tiled = jnp.broadcast_to(block[None], (copies,) + block.shape)
    return lax.all_to_all(tiled, axis, 0, 0)


def on_device(strain, counts, working, mixing, owners, offsets):
    channels, samples = strain.shape
    part = samples // 2
    seg = lax.axis_index("seg")
    grp = lax.axis_index("grp")
    side, level = grp // DEPTH, grp % DEPTH

    core = seg % 2
    fetched = lax.dynamic_slice_in_dim(mixing, core * (channels // 2), channels // 2, 0)
    fetched = lax.ppermute(fetched, "grp", ACROSS)
    valid = jnp.where(working > 0, counts, 0)
    positions = lax.broadcasted_iota(jnp.int32, strain.shape, 1)
    masked = jnp.where(positions < valid[:, None], strain, jnp.zeros_like(strain))
    first, second = masked[:, :part], masked[:, part:]
    mine = jnp.where(side == 0, first, second)

    lanes = lax.broadcasted_iota(jnp.int32, (channels, 128), 1)
    digits = jnp.where(lanes < 64, valid[:, None] >> 7, valid[:, None] & 127)
    theirs = jnp.where(side == 0, second, first)
    theirs = jnp.concatenate([theirs, digits.astype(theirs.dtype)], axis=1)
    theirs = lax.ppermute(theirs, "grp", ACROSS)
    partner = theirs[:, :part]
    high = theirs[:, part].astype(jnp.float32)
    low = theirs[:, part + 127].astype(jnp.float32)
    valid2 = jnp.concatenate([valid, (high * 128.0 + low).astype(jnp.int32)])

    def term(away, who, rows):
        at = (jnp.where(who == 0, side, 1 - side) * DEPTH + (level + away) % DEPTH) * channels
        left = lax.dynamic_slice_in_dim(mixing2, at, channels, 1)
        return jnp.dot(left, rows, preferred_element_type=jnp.float32)

    held = [(0, 0, mine), (0, 1, partner)]
    up, down = [mine, partner], [mine, partner]
    for hop in range(1, DEPTH // 2):
        for who in range(2):
            one = lax.ppermute(up[who], "grp", UP)
            two = lax.ppermute(down[who], "grp", DOWN)
            up[who], down[who] = lax.optimization_barrier((one, two))
            if hop == 1 and who == 1:
                up[who], fetched = lax.optimization_barrier((up[who], fetched))
                handed = lax.ppermute(fetched, "seg", CORES)
            if hop == 2 and who == 1:
                up[who], handed = lax.optimization_barrier((up[who], handed))
            held += [(-hop, who, up[who]), (hop, who, down[who])]
    mixing2 = jnp.concatenate(
        [mixing, jnp.where(core == 0, fetched, handed), jnp.where(core == 0, handed, fetched)]
    )
    held.append((DEPTH // 2, 0, lax.ppermute(up[0], "grp", UP)))
    held.append((DEPTH // 2, 1, lax.ppermute(down[1], "grp", DOWN)))
    coupled = term(*held[0])
    for item in held[1:]:
        coupled = coupled + term(*item)
    block = jnp.concatenate([mine, partner])

    places = side * part + lax.broadcasted_iota(jnp.int32, block.shape, 1)
    usable2 = places < valid2[:, None]
    filtered = jnp.where(usable2, block.astype(jnp.float32) - coupled, jnp.float32(0.0))

    segs = lax.axis_size("seg")
    share = ROUNDS * SRC // segs
    lanes = lax.broadcasted_iota(jnp.int32, (2 * channels, 128), 1)
    digits = jnp.where(lanes < 64, valid2[:, None] >> 7, valid2[:, None] & 127)
    marked = jnp.concatenate(
        [filtered.astype(jnp.bfloat16), digits.astype(jnp.bfloat16)], axis=1
    )
    owner = jnp.repeat(owners, SRC)[:, None]
    place = jnp.repeat(offsets, SRC)[:, None] + jnp.tile(jnp.arange(SRC), ROUNDS)[:, None]
    owner_seg, owner_grp = owner // 16, owner % 16
    place = jnp.where(owner_grp // DEPTH == side, place, place + channels)
    here = (owner_seg == seg) & (owner_grp % DEPTH == level)
    every = lax.broadcasted_iota(jnp.int32, (ROUNDS * SRC, 2 * channels), 1)
    chosen = ((every == place) & here).astype(jnp.bfloat16)
    picked = jnp.dot(chosen, marked, preferred_element_type=jnp.float32).astype(jnp.bfloat16)
    picked = picked.reshape(segs, share, part + 128)
    spread_rows = jnp.sum(lax.all_to_all(picked, "seg", 0, 0), axis=0)
    sums = jnp.sum(filtered * filtered, axis=1, keepdims=True)
    lacking = jnp.broadcast_to(sums[channels:], (channels, 128))
    lacking = jnp.concatenate([filtered[channels:], lacking], axis=1)
    spread_rows, lacking = lax.optimization_barrier((spread_rows, lacking))
    spread_rows = everyone(spread_rows, "grp").reshape(2, DEPTH, share, part + 128)
    spread_rows = jnp.sum(spread_rows, axis=1)
    source = jnp.concatenate([spread_rows[0, :, :part], spread_rows[1, :, :part]], axis=1)
    high = spread_rows[0, :, part : part + 1].astype(jnp.float32)
    low = spread_rows[0, :, part + 127 :].astype(jnp.float32)
    powers = jnp.sum(jnp.square(source.astype(jnp.float32)), axis=1, keepdims=True)
    scale = lax.rsqrt(powers / jnp.maximum(high * 128.0 + low, 1.0) + epsilon)
    coarse = scale.astype(jnp.bfloat16)
    finer = (scale - coarse.astype(jnp.float32)).astype(jnp.bfloat16)
    lanes = lax.broadcasted_iota(jnp.int32, (share, 128), 1)
    scales = jnp.where(lanes < 64, coarse, finer)
    sources = everyone(jnp.concatenate([source, scales], axis=1), "seg")
    sources = sources.reshape(ROUNDS * SRC, samples + 128)

    lacking = lax.ppermute(lacking, "grp", ACROSS)
    sums = sums[:channels] + lacking[:, part : part + 1]
    spread = jnp.sqrt(sums / jnp.maximum(valid, 1).astype(jnp.float32)[:, None] + epsilon)
    kept = (filtered[:channels] / spread).astype(jnp.bfloat16)
    returned = (lacking[:, :part] / spread).astype(jnp.bfloat16)
    whitened = jnp.concatenate(
        [jnp.where(side == 0, kept, returned), jnp.where(side == 0, returned, kept)], axis=1
    )
    return correlate(whitened, sources)


def solution(mesh):
    in_specs = (
        P(("seg", "grp"), None),
        P(("seg", "grp")),
        P(("seg", "grp")),
        P("grp", None),
        P(),
        P(),
    )
    out_specs = P(None, None, None, ("seg", "grp"))
    return jax.shard_map(
        on_device, mesh=mesh, in_specs=in_specs, out_specs=out_specs, check_vma=False
    )
```

```python
import jax
import jax.numpy as jnp
from jax import lax
from jax.experimental import pallas as pl
from jax.experimental.pallas import tpu as pltpu
from jax.sharding import PartitionSpec as P

SRC = 64
LAG = 100
ROUNDS = 2
LAGS = 201
DEPTH = 8
FINE = 13
COARSE = 8
CHUNK = 2
SPAN = FINE * COARSE

epsilon = 1e-05

CORES = [(s, s ^ 1) for s in range(16)]
ACROSS = [(a * DEPTH + z, (1 - a) * DEPTH + z) for a in range(2) for z in range(DEPTH)]
UP = [(a * DEPTH + z, a * DEPTH + (z + 1) % DEPTH) for a in range(2) for z in range(DEPTH)]
DOWN = [(a * DEPTH + z, a * DEPTH + (z - 1) % DEPTH) for a in range(2) for z in range(DEPTH)]


def correlate_kernel(
    channel_ref, source_ref, out_ref, turned_ref, left_ref, right_ref, stage_ref, sems
):
    rows = source_ref.shape[0]
    channels, samples = channel_ref.shape
    scales = source_ref[:, samples:].astype(jnp.float32)
    scale = (scales[:, :1] + scales[:, 127:]) * (1.0 / float(samples) ** 0.5)
    turned_ref[:SPAN, :] = jnp.zeros((SPAN, channels), jnp.float32)
    turned_ref[SPAN + samples :, :] = jnp.zeros((SPAN, channels), jnp.float32)
    turned_ref[SPAN : SPAN + samples, :] = channel_ref[...].astype(jnp.float32).T

    def place_sources(side):
        padded = jnp.concatenate(
            [source_ref[:, :samples].astype(jnp.float32), jnp.zeros((rows, 128), jnp.float32)],
            axis=1,
        )
        for fine in range(FINE):
            ahead = fine + (1 if side else 1 - FINE)
            moved = pltpu.roll(padded, (-ahead) % (samples + 128), axis=1) if ahead else padded
            left_ref[side, fine * rows : (fine + 1) * rows, :] = moved[:, :samples].astype(
                jnp.bfloat16
            )

    def place_channels(side):
        for coarse in range(COARSE):
            start = SPAN + FINE * (-coarse if side else coarse)
            right_ref[side, :, coarse * channels : (coarse + 1) * channels] = turned_ref[
                start : start + samples, :
            ].astype(jnp.bfloat16)

    def copies(side, begin, some):
        made = []
        for coarse in range(COARSE):
            at = (coarse if side else COARSE - 1 - coarse) * FINE + begin
            lag = at + (LAG + 1 if side else LAG + 1 - SPAN)
            skip, end = max(0, -lag), min(some, LAGS - lag)
            for r in range(ROUNDS if end > skip else 0):
                made.append(
                    pltpu.make_async_copy(
                        stage_ref.at[side, r, pl.ds(at + skip, end - skip)],
                        out_ref.at[r, pl.ds(lag + skip, end - skip)],
                        sems.at[side, r],
                    )
                )
        return made

    place_sources(0)
    place_channels(0)
    for side in range(2):
        for begin in range(0, FINE, CHUNK):
            some = min(CHUNK, FINE - begin)
            products = jnp.dot(
                left_ref[side, begin * rows : (begin + some) * rows, :],
                right_ref[side],
                preferred_element_type=jnp.float32,
            )
            scaled = (products * jnp.concatenate([scale] * some)).astype(jnp.bfloat16)
            for coarse in range(COARSE):
                for fine in range(begin, begin + some):
                    at = (coarse if side else COARSE - 1 - coarse) * FINE + fine
                    for r in range(ROUNDS):
                        top = (fine - begin) * rows + r * SRC
                        stage_ref[side, r, at] = scaled[
                            top : top + SRC, coarse * channels : (coarse + 1) * channels
                        ]
            for copy in copies(side, begin, some):
                copy.start()
        if side == 0:
            place_sources(1)
            place_channels(1)
    for side in range(2):
        for begin in range(0, FINE, CHUNK):
            for copy in copies(side, begin, min(CHUNK, FINE - begin)):
                copy.wait()


def correlate(whitened, sources):
    channels, samples = whitened.shape
    rows = sources.shape[0]
    return pl.pallas_call(
        correlate_kernel,
        out_shape=jax.ShapeDtypeStruct((ROUNDS, LAGS, SRC, channels), jnp.bfloat16),
        in_specs=[pl.BlockSpec(memory_space=pltpu.VMEM)] * 2,
        out_specs=pl.BlockSpec(memory_space=pl.ANY),
        scratch_shapes=[
            pltpu.VMEM((samples + 2 * SPAN, channels), jnp.float32),
            pltpu.VMEM((2, FINE * rows, samples), jnp.bfloat16),
            pltpu.VMEM((2, samples, COARSE * channels), jnp.bfloat16),
            pltpu.VMEM((2, ROUNDS, SPAN, SRC, channels), jnp.bfloat16),
            pltpu.SemaphoreType.DMA((2, ROUNDS)),
        ],
        compiler_params=pltpu.CompilerParams(vmem_limit_bytes=56 * 2**20),
        cost_estimate=pl.CostEstimate(
            flops=2 * LAGS * rows * channels * samples, bytes_accessed=8 * 2**20, transcendentals=0
        ),
    )(whitened, sources)


def everyone(block, axis):
    copies = lax.axis_size(axis)
    tiled = jnp.broadcast_to(block[None], (copies,) + block.shape)
    return lax.all_to_all(tiled, axis, 0, 0)


def on_device(strain, counts, working, mixing, owners, offsets):
    channels, samples = strain.shape
    part = samples // 2
    seg = lax.axis_index("seg")
    grp = lax.axis_index("grp")
    side, level = grp // DEPTH, grp % DEPTH

    core = seg % 2
    fetched = lax.dynamic_slice_in_dim(mixing, core * (channels // 2), channels // 2, 0)
    fetched = lax.ppermute(fetched, "grp", ACROSS)
    valid = jnp.where(working > 0, counts, 0)
    positions = lax.broadcasted_iota(jnp.int32, strain.shape, 1)
    masked = jnp.where(positions < valid[:, None], strain, jnp.zeros_like(strain))
    first, second = masked[:, :part], masked[:, part:]
    mine = jnp.where(side == 0, first, second)

    lanes = lax.broadcasted_iota(jnp.int32, (channels, 128), 1)
    digits = jnp.where(lanes < 64, valid[:, None] >> 7, valid[:, None] & 127)
    theirs = jnp.where(side == 0, second, first)
    theirs = jnp.concatenate([theirs, digits.astype(theirs.dtype)], axis=1)
    theirs = lax.ppermute(theirs, "grp", ACROSS)
    partner = theirs[:, :part]
    high = theirs[:, part].astype(jnp.float32)
    low = theirs[:, part + 127].astype(jnp.float32)
    valid2 = jnp.concatenate([valid, (high * 128.0 + low).astype(jnp.int32)])

    def term(away, who, rows):
        at = (jnp.where(who == 0, side, 1 - side) * DEPTH + (level + away) % DEPTH) * channels
        left = lax.dynamic_slice_in_dim(mixing2, at, channels, 1)
        return jnp.dot(left, rows, preferred_element_type=jnp.float32)

    held = [(0, 0, mine), (0, 1, partner)]
    up, down = [mine, partner], [mine, partner]
    for hop in range(1, DEPTH // 2):
        for who in range(2):
            one = lax.ppermute(up[who], "grp", UP)
            two = lax.ppermute(down[who], "grp", DOWN)
            if hop < 3 or who == 0:
                one, two = lax.optimization_barrier((one, two))
            up[who], down[who] = one, two
            if hop == 1 and who == 1:
                up[who], fetched = lax.optimization_barrier((up[who], fetched))
                handed = lax.ppermute(fetched, "seg", CORES)
            if hop == 3 and who == 0:
                up[who], handed = lax.optimization_barrier((up[who], handed))
            held += [(-hop, who, up[who]), (hop, who, down[who])]
    mixing2 = jnp.concatenate(
        [mixing, jnp.where(core == 0, fetched, handed), jnp.where(core == 0, handed, fetched)]
    )
    held.append((DEPTH // 2, 0, lax.ppermute(up[0], "grp", UP)))
    held.append((DEPTH // 2, 1, lax.ppermute(down[1], "grp", DOWN)))
    coupled = term(*held[0])
    for item in held[1:]:
        coupled = coupled + term(*item)
    block = jnp.concatenate([mine, partner])

    places = side * part + lax.broadcasted_iota(jnp.int32, block.shape, 1)
    usable2 = places < valid2[:, None]
    filtered = jnp.where(usable2, block.astype(jnp.float32) - coupled, jnp.float32(0.0))

    segs = lax.axis_size("seg")
    share = ROUNDS * SRC // segs
    lanes = lax.broadcasted_iota(jnp.int32, (2 * channels, 128), 1)
    digits = jnp.where(lanes < 64, valid2[:, None] >> 7, valid2[:, None] & 127)
    marked = jnp.concatenate(
        [filtered.astype(jnp.bfloat16), digits.astype(jnp.bfloat16)], axis=1
    )
    owner = jnp.repeat(owners, SRC)[:, None]
    place = jnp.repeat(offsets, SRC)[:, None] + jnp.tile(jnp.arange(SRC), ROUNDS)[:, None]
    owner_seg, owner_grp = owner // 16, owner % 16
    place = jnp.where(owner_grp // DEPTH == side, place, place + channels)
    here = (owner_seg == seg) & (owner_grp % DEPTH == level)
    every = lax.broadcasted_iota(jnp.int32, (ROUNDS * SRC, 2 * channels), 1)
    chosen = ((every == place) & here).astype(jnp.bfloat16)
    picked = jnp.dot(chosen, marked, preferred_element_type=jnp.float32).astype(jnp.bfloat16)
    picked = picked.reshape(segs, share, part + 128)
    spread_rows = jnp.sum(lax.all_to_all(picked, "seg", 0, 0), axis=0)
    sums = jnp.sum(filtered * filtered, axis=1, keepdims=True)
    lacking = jnp.broadcast_to(sums[channels:], (channels, 128))
    lacking = jnp.concatenate([filtered[channels:], lacking], axis=1)
    spread_rows, lacking = lax.optimization_barrier((spread_rows, lacking))
    spread_rows = everyone(spread_rows, "grp").reshape(2, DEPTH, share, part + 128)
    spread_rows = jnp.sum(spread_rows, axis=1)
    source = jnp.concatenate([spread_rows[0, :, :part], spread_rows[1, :, :part]], axis=1)
    high = spread_rows[0, :, part : part + 1].astype(jnp.float32)
    low = spread_rows[0, :, part + 127 :].astype(jnp.float32)
    powers = jnp.sum(jnp.square(source.astype(jnp.float32)), axis=1, keepdims=True)
    scale = lax.rsqrt(powers / jnp.maximum(high * 128.0 + low, 1.0) + epsilon)
    coarse = scale.astype(jnp.bfloat16)
    finer = (scale - coarse.astype(jnp.float32)).astype(jnp.bfloat16)
    lanes = lax.broadcasted_iota(jnp.int32, (share, 128), 1)
    scales = jnp.where(lanes < 64, coarse, finer)
    sources = everyone(jnp.concatenate([source, scales], axis=1), "seg")
    sources = sources.reshape(ROUNDS * SRC, samples + 128)

    lacking = lax.ppermute(lacking, "grp", ACROSS)
    sums = sums[:channels] + lacking[:, part : part + 1]
    spread = jnp.sqrt(sums / jnp.maximum(valid, 1).astype(jnp.float32)[:, None] + epsilon)
    kept = (filtered[:channels] / spread).astype(jnp.bfloat16)
    returned = (lacking[:, :part] / spread).astype(jnp.bfloat16)
    whitened = jnp.concatenate(
        [jnp.where(side == 0, kept, returned), jnp.where(side == 0, returned, kept)], axis=1
    )
    return correlate(whitened, sources)


def solution(mesh):
    in_specs = (
        P(("seg", "grp"), None),
        P(("seg", "grp")),
        P(("seg", "grp")),
        P("grp", None),
        P(),
        P(),
    )
    out_specs = P(None, None, None, ("seg", "grp"))
    return jax.shard_map(
        on_device, mesh=mesh, in_specs=in_specs, out_specs=out_specs, check_vma=False
    )
```

```python
import jax
import jax.numpy as jnp
from jax import lax
from jax.experimental import pallas as pl
from jax.experimental.pallas import tpu as pltpu
from jax.sharding import PartitionSpec as P

SRC = 64
LAG = 100
ROUNDS = 2
LAGS = 201
DEPTH = 8
FINE = 13
COARSE = 8
CHUNK = 2
SPAN = FINE * COARSE

epsilon = 1e-05

CORES = [(s, s ^ 1) for s in range(16)]
ACROSS = [(a * DEPTH + z, (1 - a) * DEPTH + z) for a in range(2) for z in range(DEPTH)]
UP = [(a * DEPTH + z, a * DEPTH + (z + 1) % DEPTH) for a in range(2) for z in range(DEPTH)]
DOWN = [(a * DEPTH + z, a * DEPTH + (z - 1) % DEPTH) for a in range(2) for z in range(DEPTH)]


def correlate_kernel(
    channel_ref,
    far_ref,
    out_ref,
    source_ref,
    turned_ref,
    left_ref,
    right_ref,
    stage_ref,
    sems,
    source_sem,
):
    rows = source_ref.shape[0]
    channels, samples = channel_ref.shape
    arriving = pltpu.make_async_copy(far_ref, source_ref, source_sem)
    arriving.start()
    turned_ref[:SPAN, :] = jnp.zeros((SPAN, channels), jnp.float32)
    turned_ref[SPAN + samples :, :] = jnp.zeros((SPAN, channels), jnp.float32)
    turned_ref[SPAN : SPAN + samples, :] = channel_ref[...].astype(jnp.float32).T

    def place_sources(side):
        padded = jnp.concatenate(
            [source_ref[:, :samples].astype(jnp.float32), jnp.zeros((rows, 128), jnp.float32)],
            axis=1,
        )
        for fine in range(FINE):
            ahead = fine + (1 if side else 1 - FINE)
            moved = pltpu.roll(padded, (-ahead) % (samples + 128), axis=1) if ahead else padded
            left_ref[side, fine * rows : (fine + 1) * rows, :] = moved[:, :samples].astype(
                jnp.bfloat16
            )

    def place_channels(side):
        for coarse in range(COARSE):
            start = SPAN + FINE * (-coarse if side else coarse)
            right_ref[side, :, coarse * channels : (coarse + 1) * channels] = turned_ref[
                start : start + samples, :
            ].astype(jnp.bfloat16)

    def copies(side, begin, some):
        made = []
        for coarse in range(COARSE):
            at = (coarse if side else COARSE - 1 - coarse) * FINE + begin
            lag = at + (LAG + 1 if side else LAG + 1 - SPAN)
            skip, end = max(0, -lag), min(some, LAGS - lag)
            for r in range(ROUNDS if end > skip else 0):
                made.append(
                    pltpu.make_async_copy(
                        stage_ref.at[side, r, pl.ds(at + skip, end - skip)],
                        out_ref.at[r, pl.ds(lag + skip, end - skip)],
                        sems.at[side, r],
                    )
                )
        return made

    place_channels(0)
    arriving.wait()
    scales = source_ref[:, samples:].astype(jnp.float32)
    scale = (scales[:, :1] + scales[:, 127:]) * (1.0 / float(samples) ** 0.5)
    place_sources(0)
    for side in range(2):
        for begin in range(0, FINE, CHUNK):
            some = min(CHUNK, FINE - begin)
            products = jnp.dot(
                left_ref[side, begin * rows : (begin + some) * rows, :],
                right_ref[side],
                preferred_element_type=jnp.float32,
            )
            scaled = (products * jnp.concatenate([scale] * some)).astype(jnp.bfloat16)
            for coarse in range(COARSE):
                for fine in range(begin, begin + some):
                    at = (coarse if side else COARSE - 1 - coarse) * FINE + fine
                    for r in range(ROUNDS):
                        top = (fine - begin) * rows + r * SRC
                        stage_ref[side, r, at] = scaled[
                            top : top + SRC, coarse * channels : (coarse + 1) * channels
                        ]
            for copy in copies(side, begin, some):
                copy.start()
        if side == 0:
            place_sources(1)
            place_channels(1)
    for side in range(2):
        for begin in range(0, FINE, CHUNK):
            for copy in copies(side, begin, min(CHUNK, FINE - begin)):
                copy.wait()


def correlate(whitened, sources):
    channels, samples = whitened.shape
    rows = sources.shape[0]
    return pl.pallas_call(
        correlate_kernel,
        out_shape=jax.ShapeDtypeStruct((ROUNDS, LAGS, SRC, channels), jnp.bfloat16),
        in_specs=[pl.BlockSpec(memory_space=pltpu.VMEM), pl.BlockSpec(memory_space=pl.ANY)],
        out_specs=pl.BlockSpec(memory_space=pl.ANY),
        scratch_shapes=[
            pltpu.VMEM(sources.shape, sources.dtype),
            pltpu.VMEM((samples + 2 * SPAN, channels), jnp.float32),
            pltpu.VMEM((2, FINE * rows, samples), jnp.bfloat16),
            pltpu.VMEM((2, samples, COARSE * channels), jnp.bfloat16),
            pltpu.VMEM((2, ROUNDS, SPAN, SRC, channels), jnp.bfloat16),
            pltpu.SemaphoreType.DMA((2, ROUNDS)),
            pltpu.SemaphoreType.DMA,
        ],
        compiler_params=pltpu.CompilerParams(vmem_limit_bytes=56 * 2**20),
        cost_estimate=pl.CostEstimate(
            flops=2 * LAGS * rows * channels * samples, bytes_accessed=8 * 2**20, transcendentals=0
        ),
    )(whitened, sources)


def everyone(block, axis):
    copies = lax.axis_size(axis)
    tiled = jnp.broadcast_to(block[None], (copies,) + block.shape)
    return lax.all_to_all(tiled, axis, 0, 0)


def on_device(strain, counts, working, mixing, owners, offsets):
    channels, samples = strain.shape
    part = samples // 2
    seg = lax.axis_index("seg")
    grp = lax.axis_index("grp")
    side, level = grp // DEPTH, grp % DEPTH

    core = seg % 2
    fetched = lax.dynamic_slice_in_dim(mixing, core * (channels // 2), channels // 2, 0)
    fetched = lax.ppermute(fetched, "grp", ACROSS)
    valid = jnp.where(working > 0, counts, 0)
    positions = lax.broadcasted_iota(jnp.int32, strain.shape, 1)
    masked = jnp.where(positions < valid[:, None], strain, jnp.zeros_like(strain))
    first, second = masked[:, :part], masked[:, part:]
    mine = jnp.where(side == 0, first, second)

    lanes = lax.broadcasted_iota(jnp.int32, (channels, 128), 1)
    digits = jnp.where(lanes < 64, valid[:, None] >> 7, valid[:, None] & 127)
    theirs = jnp.where(side == 0, second, first)
    theirs = jnp.concatenate([theirs, digits.astype(theirs.dtype)], axis=1)
    theirs = lax.ppermute(theirs, "grp", ACROSS)
    partner = theirs[:, :part]
    high = theirs[:, part].astype(jnp.float32)
    low = theirs[:, part + 127].astype(jnp.float32)
    valid2 = jnp.concatenate([valid, (high * 128.0 + low).astype(jnp.int32)])

    def term(away, who, rows):
        at = (jnp.where(who == 0, side, 1 - side) * DEPTH + (level + away) % DEPTH) * channels
        left = lax.dynamic_slice_in_dim(mixing2, at, channels, 1)
        return jnp.dot(left, rows, preferred_element_type=jnp.float32)

    held = [(0, 0, mine), (0, 1, partner)]
    up, down = [mine, partner], [mine, partner]
    for hop in range(1, DEPTH // 2):
        for who in range(2):
            one = lax.ppermute(up[who], "grp", UP)
            two = lax.ppermute(down[who], "grp", DOWN)
            if hop < 3:
                one, two = lax.optimization_barrier((one, two))
            up[who], down[who] = one, two
            if hop == 1 and who == 1:
                up[who], fetched = lax.optimization_barrier((up[who], fetched))
                handed = lax.ppermute(fetched, "seg", CORES)
            if hop == 3 and who == 0:
                up[who], handed = lax.optimization_barrier((up[who], handed))
            held += [(-hop, who, up[who]), (hop, who, down[who])]
    mixing2 = jnp.concatenate(
        [mixing, jnp.where(core == 0, fetched, handed), jnp.where(core == 0, handed, fetched)]
    )
    held.append((DEPTH // 2, 0, lax.ppermute(up[0], "grp", UP)))
    held.append((DEPTH // 2, 1, lax.ppermute(down[1], "grp", DOWN)))
    coupled = term(*held[0])
    for item in held[1:]:
        coupled = coupled + term(*item)
    block = jnp.concatenate([mine, partner])

    places = side * part + lax.broadcasted_iota(jnp.int32, block.shape, 1)
    usable2 = places < valid2[:, None]
    filtered = jnp.where(usable2, block.astype(jnp.float32) - coupled, jnp.float32(0.0))

    segs = lax.axis_size("seg")
    share = ROUNDS * SRC // segs
    lanes = lax.broadcasted_iota(jnp.int32, (2 * channels, 128), 1)
    digits = jnp.where(lanes < 64, valid2[:, None] >> 7, valid2[:, None] & 127)
    marked = jnp.concatenate(
        [filtered.astype(jnp.bfloat16), digits.astype(jnp.bfloat16)], axis=1
    )
    owner = jnp.repeat(owners, SRC)[:, None]
    place = jnp.repeat(offsets, SRC)[:, None] + jnp.tile(jnp.arange(SRC), ROUNDS)[:, None]
    owner_seg, owner_grp = owner // 16, owner % 16
    place = jnp.where(owner_grp // DEPTH == side, place, place + channels)
    here = (owner_seg == seg) & (owner_grp % DEPTH == level)
    every = lax.broadcasted_iota(jnp.int32, (ROUNDS * SRC, 2 * channels), 1)
    chosen = ((every == place) & here).astype(jnp.bfloat16)
    picked = jnp.dot(chosen, marked, preferred_element_type=jnp.float32).astype(jnp.bfloat16)
    picked = picked.reshape(segs, share, part + 128)
    spread_rows = jnp.sum(lax.all_to_all(picked, "seg", 0, 0), axis=0)
    sums = jnp.sum(filtered * filtered, axis=1, keepdims=True)
    lacking = jnp.broadcast_to(sums[channels:], (channels, 128))
    lacking = jnp.concatenate([filtered[channels:], lacking], axis=1)
    spread_rows, lacking = lax.optimization_barrier((spread_rows, lacking))
    spread_rows = everyone(spread_rows, "grp").reshape(2, DEPTH, share, part + 128)
    spread_rows = jnp.sum(spread_rows, axis=1)
    source = jnp.concatenate([spread_rows[0, :, :part], spread_rows[1, :, :part]], axis=1)
    high = spread_rows[0, :, part : part + 1].astype(jnp.float32)
    low = spread_rows[0, :, part + 127 :].astype(jnp.float32)
    powers = jnp.sum(jnp.square(source.astype(jnp.float32)), axis=1, keepdims=True)
    scale = lax.rsqrt(powers / jnp.maximum(high * 128.0 + low, 1.0) + epsilon)
    coarse = scale.astype(jnp.bfloat16)
    finer = (scale - coarse.astype(jnp.float32)).astype(jnp.bfloat16)
    lanes = lax.broadcasted_iota(jnp.int32, (share, 128), 1)
    scales = jnp.where(lanes < 64, coarse, finer)
    sources = everyone(jnp.concatenate([source, scales], axis=1), "seg")
    sources = sources.reshape(ROUNDS * SRC, samples + 128)

    lacking = lax.ppermute(lacking, "grp", ACROSS)
    sums = sums[:channels] + lacking[:, part : part + 1]
    spread = jnp.sqrt(sums / jnp.maximum(valid, 1).astype(jnp.float32)[:, None] + epsilon)
    kept = (filtered[:channels] / spread).astype(jnp.bfloat16)
    returned = (lacking[:, :part] / spread).astype(jnp.bfloat16)
    whitened = jnp.concatenate(
        [jnp.where(side == 0, kept, returned), jnp.where(side == 0, returned, kept)], axis=1
    )
    return correlate(whitened, sources)


def solution(mesh):
    in_specs = (
        P(("seg", "grp"), None),
        P(("seg", "grp")),
        P(("seg", "grp")),
        P("grp", None),
        P(),
        P(),
    )
    out_specs = P(None, None, None, ("seg", "grp"))
    return jax.shard_map(
        on_device, mesh=mesh, in_specs=in_specs, out_specs=out_specs, check_vma=False
    )
```
